128 devices in a mesh: prow: 8 (over y, core), pcol: 16 (over x, z).
Axes of the slice: x: 4, y: 4, z: 4, core: 2. Of those that a mesh axis runs over, the one named last changes fastest.
Arguments:
- right_side: float32 [8, 128, 128, 128], P(None, ('prow', 'pcol')), may hold values from -6 to 6
- blocks: bfloat16 [7, 128, 64, 128, 128], P(None, 'prow', 'pcol'), may hold values from -0.0625 to 0.0625
- pattern: int32 [7, 128, 64], P(None, 'prow', 'pcol'), may hold values from 0 to 895, as said below
- diag_inverse: bfloat16 [8, 128, 128, 128], P(None, ('prow', 'pcol')), may hold values from -0.1 to 2, as said below
Outputs:
- forward_out: float32 [8, 128, 128, 128], P(None, ('prow', 'pcol'))
- solution: float32 [8, 128, 128, 128], P(None, ('prow', 'pcol'))
The draws below stay inside these ranges and needn't reach their ends.
Inputs may be any that keep to these rules, and one draw needn't show every extreme that they name: pattern[l, t, k] names a block row of a level below l + 1; with j = pattern[l, t, k], (j % 128) % 16 equals k // 4; slot k with k % 4 = 0 names a block row of level l. Each diag_inverse[l, t] is lower triangular with a positive diagonal.
All inputs are finite; a program needn't handle non-finite values.
Results may differ from the reference program's by a relative error of at most 0.04.
Values may be sent and summed in bfloat16 or wider, within the bound.
No kernel may reach another device: no remote copies, remote signals or barrier semaphores. Data moves between devices by JAX's collectives and lax.ppermute only.
A program may use at most 128 MiB of HBM per device.

```python
import jax
import jax.numpy as jnp
from jax import lax

BS = 128
RHS = 128
LEV = 8
PD = 1
KC = 4
NROW = 8
NCOL = 16
LB = 128
K = 64


def draw_pattern(key, part):
    key_level, key_offset = jax.random.split(jax.random.fold_in(key, 11))
    stored = jnp.arange(1, LEV, dtype=jnp.int32)[:, None, None, None]
    random_level = jax.random.randint(key_level, (LEV - 1, LB, NCOL, KC), 0, 2 ** 30) % stored
    slot_index = jnp.arange(KC, dtype=jnp.int32)[None, None, None, :]
    level_pick = jnp.where(slot_index == 0, stored - 1, random_level)
    combos = NROW * PD
    offset_pick = jax.random.randint(key_offset, (LEV - 1, LB, NCOL, 1), 0, combos)
    row_first = jnp.arange(LB, dtype=jnp.int32)[None, :, None, None] == 0
    offset_pick = jnp.where(row_first, combos - 1, offset_pick)
    combo = (offset_pick + slot_index) % combos
    prow_pick = combo // PD
    panel_pick = combo % PD
    column_group = jnp.arange(NCOL, dtype=jnp.int32)[None, None, :, None]
    within = (prow_pick * NCOL + column_group) * PD + panel_pick
    result = level_pick * LB + within
    return result.reshape(LEV - 1, LB, NCOL * KC).astype(jnp.int32)


def draw_diag_inverse(key, part):
    key_diag, key_off = jax.random.split(jax.random.fold_in(key, 23))
    lower = jnp.arange(BS)[:, None] > jnp.arange(BS)[None, :]
    ident = jnp.arange(BS)[:, None] == jnp.arange(BS)[None, :]
    diagonal_part = jax.random.uniform(key_diag, (LEV, LB, BS, 1), jnp.float32, 0.7, 1.4)
    off_part = jax.random.uniform(key_off, (LEV, LB, BS, BS), jnp.float32, -0.099, 0.099)
    result = jnp.where(ident, diagonal_part, jnp.where(lower, off_part, 0.0))
    return result.astype(jnp.bfloat16)


def level_of(own_key, dims, shards, low, largest):
    factor_of = 1.0
    for position, blocks in shards:
        steps = jax.random.uniform(jax.random.fold_in(jax.random.fold_in(own_key, 6), position), (blocks,), jnp.float32, low / len(shards), largest / len(shards))
        factor_of = factor_of * jnp.repeat(jnp.exp(steps), dims[position] // blocks).reshape((-1,) + (1,) * (len(dims) - 1 - position))
    return factor_of


def bell_draw(rng, dims, spread, most, cuts=(), held_as=jnp.bfloat16):
    values = spread * jax.random.normal(rng, dims, jnp.float32)
    if cuts:
        values = values * level_of(rng, dims, cuts, -0.22, 0.18)
    return jnp.clip(values, -most, most).astype(held_as)


def setup_inputs(seed: int = 0) -> dict:
    streams_of = jax.random.split(jax.random.key(seed), 5)
    return {
        "right_side": bell_draw(streams_of[0], (LEV, LB, BS, RHS), 1.0, 6.0, ((1, 128),), jnp.float32),
        "blocks": bell_draw(streams_of[1], (LEV - 1, LB, K, BS, BS), (K * BS) ** -0.5, 0.0625, ((1, 8), (2, 16))),
        "pattern": draw_pattern(jax.random.fold_in(streams_of[4], 71), 0),
        "diag_inverse": draw_diag_inverse(jax.random.fold_in(streams_of[4], 71), 0),
    }


def reference(right_side, blocks, pattern, diag_inverse):
    solved = jnp.zeros((LEV * LB, BS, RHS), jnp.bfloat16)
    forward_list = []
    for level_at in range(LEV):
        if level_at == 0:
            lower_in = right_side[0].astype(jnp.bfloat16)
        else:
            def row_sum(row_pair, solved=solved):
                row_blocks, row_slots = row_pair
                gathered = jnp.take(solved, row_slots, axis=0).astype(jnp.float32)
                return jnp.einsum("qab,qbr->ar", row_blocks.astype(jnp.float32), gathered)

            sums = lax.map(row_sum, (blocks[level_at - 1], pattern[level_at - 1]))
            lower_in = (right_side[level_at] - sums).astype(jnp.bfloat16)
        forward_out = jnp.einsum("tab,tbr->tar", diag_inverse[level_at].astype(jnp.float32), lower_in.astype(jnp.float32))
        forward_list.append(forward_out)
        solved = lax.dynamic_update_slice_in_dim(solved, forward_out.astype(jnp.bfloat16), level_at * LB, 0)
    back_sums = jnp.zeros((LEV * LB, BS, RHS), jnp.float32)
    solution_list = [None] * LEV
    for level_at in reversed(range(LEV)):
        upper_in = (forward_list[level_at] - back_sums[level_at * LB:(level_at + 1) * LB]).astype(jnp.bfloat16)
        solution = jnp.einsum("tba,tbr->tar", diag_inverse[level_at].astype(jnp.float32), upper_in.astype(jnp.float32))
        solution_list[level_at] = solution
        if level_at > 0:
            level_blocks = blocks[level_at - 1]
            level_slots = pattern[level_at - 1]
            panel_x = solution.astype(jnp.bfloat16)

            def add_row(row_at, running, level_blocks=level_blocks, level_slots=level_slots, panel_x=panel_x):
                row_blocks = lax.dynamic_index_in_dim(level_blocks, row_at, 0, keepdims=False).astype(jnp.float32)
                row_slots = lax.dynamic_index_in_dim(level_slots, row_at, 0, keepdims=False)
                row_panel = lax.dynamic_index_in_dim(panel_x, row_at, 0, keepdims=False).astype(jnp.float32)
                return running.at[row_slots].add(jnp.einsum("qba,br->qar", row_blocks, row_panel))

            back_sums = lax.fori_loop(0, LB, add_row, back_sums)
    return jnp.stack(forward_list), jnp.stack(solution_list)
```

```python
import functools

import jax
import jax.numpy as jnp
from jax import lax
from jax.experimental import pallas as pl
from jax.experimental.pallas import tpu as pltpu
from jax.sharding import PartitionSpec as P

F32 = jnp.float32
BF16 = jnp.bfloat16
VM = pl.BlockSpec(memory_space=pltpu.VMEM)
SM = pl.BlockSpec(memory_space=pltpu.SMEM)
ANY = pl.BlockSpec(memory_space=pl.ANY)
CHUNKS = 4


def params(mib):
    return pltpu.CompilerParams(vmem_limit_bytes=mib * 1024 * 1024)


def in_vmem(x):
    return pltpu.with_memory_space_constraint(x, pltpu.VMEM)


def dot(a, b):
    return jnp.dot(a, b, preferred_element_type=F32)


def total_of(ref):
    total = ref[0].astype(F32)
    for i in range(1, ref.shape[0]):
        total = total + ref[i].astype(F32)
    return total


def diag_forward_kernel(level, *refs):
    if level:
        parts_ref, right_ref, diag_ref, fwd_in, fwd_ref, fwd_t_in, fwd_t_ref, send_ref = (
            refs[0], refs[1], refs[2], refs[3], refs[5], refs[4], refs[6], refs[7])
        lower_in = right_ref[level, 0] - total_of(parts_ref)
    else:
        right_ref, diag_ref, fwd_ref, fwd_t_ref, send_ref = refs
        lower_in = right_ref[0, 0]
    out = dot(diag_ref[level, 0], lower_in.astype(BF16))
    rounded = out.astype(BF16)
    for i in range(send_ref.shape[0]):
        send_ref[i] = rounded
    fwd_ref[level, 0] = out
    fwd_t_ref[level] = out.T


def forward_sums_kernel(level, first, *refs):
    if first:
        slots, new_ref, blocks_hbm, panels_ref, out_ref, held, sems = refs
    else:
        slots, new_ref, blocks_hbm, _, panels_ref, out_ref, held, sems = refs
    rows, per_row = held.shape[0], held.shape[1]
    step = rows // CHUNKS
    copies = []
    for c in range(CHUNKS):
        part = pl.ds(c * step, step)
        copy = pltpu.make_async_copy(blocks_hbm.at[level - 1, part], held.at[part], sems.at[c])
        copy.start()
        copies.append(copy)
    news = new_ref.shape[0]
    panels_ref[(level - 1) * news : level * news] = new_ref[...]
    for c in range(CHUNKS):
        copies[c].wait()
        for t in range(c * step, (c + 1) * step):
            base = ((level - 1) * rows + t) * per_row
            left = jnp.concatenate([held[t, q] for q in range(per_row)], axis=1)
            right = jnp.concatenate([panels_ref[slots[base + q]] for q in range(per_row)], axis=0)
            out_ref[t] = dot(left, right).astype(BF16)


def backward_diag(level, first, last, *refs):
    refs = list(refs)
    parts_ref = None if first else refs.pop(0)
    fwd_t_ref, diag_ref = refs.pop(0), refs.pop(0)
    if not first:
        refs.pop(0)
    out_ref = refs.pop(0)
    upper_t = fwd_t_ref[level]
    if parts_ref is not None:
        upper_t = upper_t - total_of(parts_ref)
    out_t = dot(upper_t.astype(BF16), diag_ref[level, 0])
    if not last:
        send_ref = refs.pop(0)
        rounded = out_t.astype(BF16)
        for i in range(send_ref.shape[0]):
            send_ref[i] = rounded
    out_ref[level, 0] = out_t.T


def backward_sums_kernel(level, first, *refs):
    if first:
        slots, panels_ref, blocks_hbm, acc_ref, out_ref, held, sems = refs
    else:
        slots, panels_ref, blocks_hbm, _, acc_ref, out_ref, held, sems = refs
    rows, per_row = held.shape[0], held.shape[1]
    width = held.shape[3]
    step = rows // CHUNKS
    copies = []
    for c in range(CHUNKS):
        part = pl.ds(c * step, step)
        copy = pltpu.make_async_copy(blocks_hbm.at[level - 1, part], held.at[part], sems.at[c])
        copy.start()
        copies.append(copy)
    if first:
        acc_ref[...] = jnp.zeros_like(acc_ref)
    for c in range(CHUNKS):
        copies[c].wait()
        for t in range(c * step, (c + 1) * step):
            base = ((level - 1) * rows + t) * per_row
            right = jnp.concatenate([held[t, q] for q in range(per_row)], axis=1)
            terms = dot(panels_ref[t], right)
            for q in range(per_row):
                at = slots[base + q]
                acc_ref[at] = acc_ref[at] + terms[:, q * width : (q + 1) * width]
    news = out_ref.shape[0]
    out_ref[...] = acc_ref[(level - 1) * news : level * news].astype(BF16)


def per_device(right_side, blocks, pattern, diag_inverse):
    levels, panels_dev, order, width = right_side.shape
    rows, per_row = blocks.shape[1], blocks.shape[2]
    row_groups = lax.axis_size("prow")
    col_groups = lax.axis_size("pcol")
    level_rows = panels_dev * row_groups * col_groups
    within = pattern % level_rows
    slots = (pattern // level_rows) * row_groups + within // (level_rows // row_groups)
    slots = slots.reshape(-1)
    held = pltpu.VMEM((rows, per_row, order, order), BF16)
    sems = pltpu.SemaphoreType.DMA((CHUNKS,))

    full = pltpu.VMEM((levels, panels_dev, order, width), F32)
    fwd_t_shape = pltpu.VMEM((levels, width, order), F32)
    send_y = pltpu.VMEM((row_groups, order, width), BF16)
    send_xz = pltpu.VMEM((col_groups, width, order), BF16)
    sums_f = pltpu.VMEM((rows, order, width), BF16)
    panels_shape = pltpu.VMEM(((levels - 1) * row_groups, order, width), BF16)
    acc_shape = pltpu.VMEM(((levels - 1) * row_groups, width, order), F32)
    right_side, diag_inverse = in_vmem(right_side), in_vmem(diag_inverse)

    fwd, fwd_t, send = pl.pallas_call(
        functools.partial(diag_forward_kernel, 0),
        in_specs=[VM, VM],
        out_specs=[VM, VM, VM],
        out_shape=[full, fwd_t_shape, send_y],
        compiler_params=params(8),
        name="forward_diag_0",
    )(right_side, diag_inverse)
    panels = None
    for level in range(1, levels):
        new = lax.all_to_all(send, "prow", 0, 0, tiled=True)
        first = panels is None
        panels, parts = pl.pallas_call(
            functools.partial(forward_sums_kernel, level, first),
            in_specs=[SM, VM, ANY] + ([] if first else [VM]),
            out_specs=[VM, VM],
            out_shape=[panels_shape, sums_f],
            scratch_shapes=[held, sems],
            input_output_aliases={} if first else {3: 0},
            compiler_params=params(16),
            name="forward_sums",
        )(*([slots, in_vmem(new), blocks] + ([] if first else [in_vmem(panels)])))
        parts = lax.all_to_all(parts, "pcol", 0, 0, tiled=True)
        fwd, fwd_t, send = pl.pallas_call(
            functools.partial(diag_forward_kernel, level),
            in_specs=[VM, VM, VM, VM, VM],
            out_specs=[VM, VM, VM],
            out_shape=[full, fwd_t_shape, send_y],
            input_output_aliases={3: 0, 4: 1},
            compiler_params=params(8),
            name="forward_diag",
        )(in_vmem(parts), right_side, diag_inverse, in_vmem(fwd), in_vmem(fwd_t))
    out = acc = parts = None
    for level in reversed(range(levels)):
        first, last = level == levels - 1, level == 0
        made = pl.pallas_call(
            functools.partial(backward_diag, level, first, last),
            in_specs=([] if first else [VM]) + [VM, VM] + ([] if first else [VM]),
            out_specs=[VM] if last else [VM, VM],
            out_shape=[full] if last else [full, send_xz],
            input_output_aliases={} if first else {3: 0},
            compiler_params=params(8),
            name="backward_diag",
        )(*(([] if first else [in_vmem(parts)]) + [in_vmem(fwd_t), diag_inverse] + ([] if first else [in_vmem(out)])))
        out = made[0]
        if last:
            break
        gathered = lax.all_to_all(made[1], "pcol", 0, 0, tiled=True)
        acc, parts = pl.pallas_call(
            functools.partial(backward_sums_kernel, level, first),
            in_specs=[SM, VM, ANY] + ([] if first else [VM]),
            out_specs=[VM, VM],
            out_shape=[acc_shape, send_y],
            scratch_shapes=[held, sems],
            input_output_aliases={} if first else {3: 0},
            compiler_params=params(24),
            name="backward_sums",
        )(*([slots, in_vmem(gathered), blocks] + ([] if first else [in_vmem(acc)])))
        parts = lax.all_to_all(parts, "prow", 0, 0, tiled=True)
    return fwd, out


def solution(mesh):
    in_specs = (
        P(None, ("prow", "pcol"), None, None),
        P(None, "prow", "pcol", None, None),
        P(None, "prow", "pcol"),
        P(None, ("prow", "pcol"), None, None),
    )
    out_specs = (P(None, ("prow", "pcol"), None, None), P(None, ("prow", "pcol"), None, None))
    return jax.shard_map(
        per_device, mesh=mesh, in_specs=in_specs, out_specs=out_specs, check_vma=False
    )
```

```python
import functools

import jax
import jax.numpy as jnp
from jax import lax
from jax.experimental import pallas as pl
from jax.experimental.pallas import tpu as pltpu
from jax.sharding import PartitionSpec as P

F32 = jnp.float32
BF16 = jnp.bfloat16
VM = pl.BlockSpec(memory_space=pltpu.VMEM)
SM = pl.BlockSpec(memory_space=pltpu.SMEM)
ANY = pl.BlockSpec(memory_space=pl.ANY)


def params(mib):
    return pltpu.CompilerParams(vmem_limit_bytes=mib * 1024 * 1024)


def in_vmem(x):
    return pltpu.with_memory_space_constraint(x, pltpu.VMEM)


def in_hbm(x):
    return pltpu.with_memory_space_constraint(x, pltpu.HBM)


def dot(a, b):
    return jnp.dot(a, b, preferred_element_type=F32)


def total_of(ref):
    total = ref[0].astype(F32)
    for i in range(1, ref.shape[0]):
        total = total + ref[i].astype(F32)
    return total


def finish_forward(level, lower_in, diag, fwd_ref, fwd_t_ref, *send):
    out = dot(diag, lower_in.astype(BF16))
    for send_ref in send:
        send_ref[...] = out.astype(BF16)
    fwd_ref[level, 0] = out
    fwd_t_ref[level] = out.T


def first_diag_kernel(right_hbm, diag_hbm, fwd_ref, fwd_t_ref, send_ref, right, diag, sems):
    copies = [
        pltpu.make_async_copy(right_hbm.at[0, 0], right, sems.at[0]),
        pltpu.make_async_copy(diag_hbm.at[0, 0], diag, sems.at[1]),
    ]
    for copy in copies:
        copy.start()
    for copy in copies:
        copy.wait()
    finish_forward(0, right[...], diag[...], fwd_ref, fwd_t_ref, send_ref)


def forward_diag_kernel(level, parts_ref, right_ref, diag_ref, fwd_in, fwd_t_in, fwd_ref, fwd_t_ref, *send):
    lower_in = right_ref[level, 0] - total_of(parts_ref)
    finish_forward(level, lower_in, diag_ref[level, 0], fwd_ref, fwd_t_ref, *send)


def row_sums(slots, base, blocks, panels_ref, out_ref, t):
    per_row = blocks.shape[0]
    left = jnp.concatenate([blocks[q] for q in range(per_row)], axis=1)
    right = jnp.concatenate([panels_ref[slots[base + q]] for q in range(per_row)], axis=0)
    out_ref[t] = dot(left, right).astype(BF16)


def pack_kernel(*refs):
    for i, ref in enumerate(refs[:-1]):
        refs[-1][i] = ref[...]


def keep_panels(at, even_ref, odd_ref, panels_ref):
    for i in range(even_ref.shape[0]):
        panels_ref[at + 2 * i] = even_ref[i]
        panels_ref[at + 2 * i + 1] = odd_ref[i]


def first_sums_kernel(slots, even_ref, odd_ref, blocks_hbm, panels_ref, out_ref, held, sems):
    rows, per_row = held.shape[:2]
    chunks = sems.shape[0]
    step = rows // chunks
    copies = []
    for c in range(chunks):
        part = pl.ds(c * step, step)
        copies.append(pltpu.make_async_copy(blocks_hbm.at[0, part], held.at[part], sems.at[c]))
        copies[c].start()
    keep_panels(0, even_ref, odd_ref, panels_ref)
    for c in range(chunks):
        copies[c].wait()
        for t in range(c * step, (c + 1) * step):
            row_sums(slots, t * per_row, held.at[t], panels_ref, out_ref, t)


def forward_sums_kernel(level, slots, even_ref, odd_ref, blocks_ref, panels_in, panels_ref, out_ref):
    rows, per_row = blocks_ref.shape[1:3]
    keep_panels((level - 1) * 2 * even_ref.shape[0], even_ref, odd_ref, panels_ref)
    for t in range(rows):
        base = ((level - 1) * rows + t) * per_row
        row_sums(slots, base, blocks_ref.at[level - 1, t], panels_ref, out_ref, t)


def backward_diag(level, first, last, count, *refs):
    refs = list(refs)
    parts = [] if first else [refs.pop(0) for _ in range(count)]
    fwd_t_ref, diag_ref = refs.pop(0), refs.pop(0)
    if not first:
        refs.pop(0)
    out_ref = refs.pop(0)
    upper_t = fwd_t_ref[level]
    if parts:
        total = parts[0][...]
        for ref in parts[1:]:
            total = total + ref[...].astype(F32)
        upper_t = upper_t - total
    out_t = dot(upper_t.astype(BF16), diag_ref[level, 0])
    if not last:
        send_ref = refs.pop(0)
        rounded = out_t.astype(BF16)
        for i in range(send_ref.shape[0]):
            send_ref[i] = rounded
    out_ref[level, 0] = out_t.T


def backward_sums_kernel(level, first, last, slots, panels_ref, blocks_ref, *refs):
    rows, per_row = blocks_ref.shape[1:3]
    width = blocks_ref.shape[4]
    if last:
        acc_in, even_ref, odd_ref, acc_ref = refs
        acc_ref[...] = acc_in[: acc_ref.shape[0]]
    else:
        acc_ref, even_ref, odd_ref = refs[-3:]
    if first:
        acc_ref[...] = jnp.zeros_like(acc_ref)
    for t in range(rows):
        base = ((level - 1) * rows + t) * per_row
        right = jnp.concatenate([blocks_ref[level - 1, t, q] for q in range(per_row)], axis=1)
        terms = dot(panels_ref[t], right)
        for q in range(per_row):
            at = slots[base + q]
            acc_ref[at] = acc_ref[at] + terms[:, q * width : (q + 1) * width]
    count = even_ref.shape[0]
    for i in range(count):
        at = (level - 1) * 2 * count + 2 * i
        even_ref[i] = acc_ref[at]
        odd_ref[i] = acc_ref[at + 1].astype(BF16)


def pair_kernel(even_ref, got_ref, own_ref, *send):
    own_ref[...] = even_ref[0] + got_ref[0].astype(F32)
    for i, ref in enumerate(send):
        ref[...] = (even_ref[i + 1] + got_ref[i + 1].astype(F32)).astype(BF16)


def swap(x, step):
    size = lax.axis_size("prow")
    return in_vmem(lax.ppermute(x, "prow", [(i, i ^ step) for i in range(size)]))


def per_device(right_side, blocks, pattern, diag_inverse):
    levels, panels_dev, order, width = right_side.shape
    rows, per_row = blocks.shape[1], blocks.shape[2]
    row_groups = lax.axis_size("prow")
    col_groups = lax.axis_size("pcol")
    level_rows = panels_dev * row_groups * col_groups
    within = pattern % level_rows
    home = (within // (level_rows // row_groups)) ^ lax.axis_index("prow")
    slots = (pattern // level_rows) * row_groups + home
    slots = slots.reshape(-1)
    full = pltpu.VMEM((levels, panels_dev, order, width), F32)
    fwd_t_shape = pltpu.VMEM((levels, width, order), F32)
    one = pltpu.VMEM((order, width), BF16)
    half = row_groups // 2
    steps = [2 * i for i in range(1, half)]
    evens_f = pltpu.VMEM((half, order, width), BF16)
    evens_b = pltpu.VMEM((half, width, order), F32)
    odds_b = pltpu.VMEM((half, width, order), BF16)
    send_xz = pltpu.VMEM((col_groups, width, order), BF16)
    sums_f = pltpu.VMEM((rows, order, width), BF16)
    panels_shape = pltpu.VMEM(((levels - 1) * row_groups, order, width), BF16)
    acc_shape = pltpu.VMEM(((levels - 1) * row_groups, width, order), F32)

    fwd, fwd_t, send = pl.pallas_call(
        first_diag_kernel,
        in_specs=[ANY, ANY],
        out_specs=[VM, VM, VM],
        out_shape=[full, fwd_t_shape, one],
        scratch_shapes=[
            pltpu.VMEM((order, width), F32),
            pltpu.VMEM((order, order), BF16),
            pltpu.SemaphoreType.DMA((2,)),
        ],
        compiler_params=params(8),
        name="first_diag",
    )(in_hbm(right_side), in_hbm(diag_inverse))
    blocks_hbm = in_hbm(blocks)
    blocks, right_side, diag_inverse = in_vmem(blocks), in_vmem(right_side), in_vmem(diag_inverse)
    panels = None
    for level in range(1, levels):
        last = level == levels - 1
        even = pl.pallas_call(
            pack_kernel,
            in_specs=[VM] * half,
            out_specs=VM,
            out_shape=evens_f,
            compiler_params=params(2),
            name="pack",
        )(in_vmem(send), *[swap(send, step) for step in steps])
        odd = swap(even, 1)
        even = in_vmem(even)
        if level == 1:
            panels, parts = pl.pallas_call(
                first_sums_kernel,
                in_specs=[SM, VM, VM, ANY],
                out_specs=[VM, VM],
                out_shape=[panels_shape, sums_f],
                scratch_shapes=[
                    pltpu.VMEM((rows, per_row, order, order), BF16),
                    pltpu.SemaphoreType.DMA((4,)),
                ],
                compiler_params=params(8),
                name="first_sums",
            )(slots, even, odd, blocks_hbm)
        else:
            panels, parts = pl.pallas_call(
                functools.partial(forward_sums_kernel, level),
                in_specs=[SM, VM, VM, VM, VM],
                out_specs=[VM, VM],
                out_shape=[panels_shape, sums_f],
                input_output_aliases={4: 0},
                compiler_params=params(8),
                name="forward_sums",
            )(slots, even, odd, blocks, in_vmem(panels))
        parts = in_vmem(lax.all_to_all(parts, "pcol", 0, 0, tiled=True))
        made = pl.pallas_call(
            functools.partial(forward_diag_kernel, level),
            in_specs=[VM, VM, VM, VM, VM],
            out_specs=[VM, VM] if last else [VM, VM, VM],
            out_shape=[full, fwd_t_shape] + ([] if last else [one]),
            input_output_aliases={3: 0, 4: 1},
            compiler_params=params(8),
            name="forward_diag",
        )(parts, right_side, diag_inverse, in_vmem(fwd), in_vmem(fwd_t))
        fwd, fwd_t, send = made[0], made[1], made[-1]
    out = acc = parts = None
    for level in reversed(range(levels)):
        first, last = level == levels - 1, level == 0
        made = pl.pallas_call(
            functools.partial(backward_diag, level, first, last, half),
            in_specs=([] if first else [VM] * half) + [VM, VM] + ([] if first else [VM]),
            out_specs=[VM] if last else [VM, VM],
            out_shape=[full] if last else [full, send_xz],
            input_output_aliases={} if first else {half + 2: 0},
            compiler_params=params(8),
            name="backward_diag",
        )(*(([] if first else parts) + [in_vmem(fwd_t), diag_inverse] + ([] if first else [in_vmem(out)])))
        out = made[0]
        if last:
            break
        gathered = in_vmem(lax.all_to_all(made[1], "pcol", 0, 0, tiled=True))
        done = level == 1
        made = pl.pallas_call(
            functools.partial(backward_sums_kernel, level, first, done),
            in_specs=[SM, VM, VM] + ([] if first else [VM]),
            out_specs=[VM, VM] if done else [VM, VM, VM],
            out_shape=([] if done else [acc_shape]) + [evens_b, odds_b],
            scratch_shapes=[pltpu.VMEM((row_groups, width, order), F32)] if done else [],
            input_output_aliases={} if first or done else {3: 0},
            compiler_params=params(8),
            name="backward_sums",
        )(*([slots, gathered, blocks] + ([] if first else [in_vmem(acc)])))
        acc = made[0]
        made = pl.pallas_call(
            pair_kernel,
            in_specs=[VM, VM],
            out_specs=[VM] * half,
            out_shape=[pltpu.VMEM((width, order), F32)] + [pltpu.VMEM((width, order), BF16)] * (half - 1),
            compiler_params=params(2),
            name="pair",
        )(in_vmem(made[-2]), swap(made[-1], 1))
        parts = [in_vmem(made[0])] + [swap(x, step) for x, step in zip(made[1:], steps)]
    return fwd, out


def solution(mesh):
    in_specs = (
        P(None, ("prow", "pcol"), None, None),
        P(None, "prow", "pcol", None, None),
        P(None, "prow", "pcol"),
        P(None, ("prow", "pcol"), None, None),
    )
    out_specs = (P(None, ("prow", "pcol"), None, None), P(None, ("prow", "pcol"), None, None))
    return jax.shard_map(
        per_device, mesh=mesh, in_specs=in_specs, out_specs=out_specs, check_vma=False
    )
```

```python
import functools

import jax
import jax.numpy as jnp
from jax import lax
from jax.experimental import pallas as pl
from jax.experimental.pallas import tpu as pltpu
from jax.sharding import PartitionSpec as P

F32 = jnp.float32
BF16 = jnp.bfloat16
VM = pl.BlockSpec(memory_space=pltpu.VMEM)
ANY = pl.BlockSpec(memory_space=pl.ANY)


def params(mib):
    return pltpu.CompilerParams(vmem_limit_bytes=mib * 1024 * 1024)


def in_vmem(x):
    return pltpu.with_memory_space_constraint(x, pltpu.VMEM)


def in_hbm(x):
    return pltpu.with_memory_space_constraint(x, pltpu.HBM)


def dot(a, b):
    return jnp.dot(a, b, preferred_element_type=F32)


def total_of(ref):
    total = ref[0].astype(F32)
    for i in range(1, ref.shape[0]):
        total = total + ref[i].astype(F32)
    return total


def finish_forward(level, lower_in, diag, fwd_ref, fwd_t_ref, *send):
    out = dot(diag, lower_in.astype(BF16))
    for send_ref in send:
        send_ref[...] = out.astype(BF16)
    fwd_ref[level, 0] = out
    fwd_t_ref[level] = out.T


def first_diag_kernel(right_hbm, diag_hbm, fwd_ref, fwd_t_ref, send_ref, right, diag, sems):
    copies = [
        pltpu.make_async_copy(right_hbm.at[0, 0], right, sems.at[0]),
        pltpu.make_async_copy(diag_hbm.at[0, 0], diag, sems.at[1]),
    ]
    for copy in copies:
        copy.start()
    for copy in copies:
        copy.wait()
    finish_forward(0, right[...], diag[...], fwd_ref, fwd_t_ref, send_ref)


def forward_diag_kernel(level, parts_ref, right_ref, diag_ref, fwd_in, fwd_t_in, fwd_ref, fwd_t_ref, *send):
    lower_in = right_ref[level, 0] - total_of(parts_ref)
    finish_forward(level, lower_in, diag_ref[level, 0], fwd_ref, fwd_t_ref, *send)


def row_sums(slots, level, blocks, panels_ref, out_ref, t):
    per_row = blocks.shape[0]
    left = jnp.concatenate([blocks[q] for q in range(per_row)], axis=1)
    at = [slots[level - 1, t * per_row + q] for q in range(per_row)]
    right = jnp.concatenate([panels_ref[i] for i in at], axis=0)
    out_ref[t] = dot(left, right).astype(BF16)


def pack_kernel(order, own_ref, *refs):
    refs[-1][0] = own_ref[...]
    for i, ref in zip(order, refs[:-1]):
        refs[-1][i] = ref[...]


def keep_panels(at, even_ref, odd_ref, panels_ref):
    for i in range(even_ref.shape[0]):
        panels_ref[at + 2 * i] = even_ref[i]
        panels_ref[at + 2 * i + 1] = odd_ref[i]


def first_sums_kernel(slots, even_ref, odd_ref, blocks_hbm, panels_ref, out_ref, held, sems):
    rows, per_row = held.shape[:2]
    chunks = sems.shape[0]
    step = rows // chunks
    copies = []
    for c in range(chunks):
        part = pl.ds(c * step, step)
        copies.append(pltpu.make_async_copy(blocks_hbm.at[0, part], held.at[part], sems.at[c]))
        copies[c].start()
    keep_panels(0, even_ref, odd_ref, panels_ref)
    for c in range(chunks):
        copies[c].wait()
        for t in range(c * step, (c + 1) * step):
            row_sums(slots, 1, held.at[t], panels_ref, out_ref, t)


def forward_sums_kernel(level, slots, even_ref, odd_ref, blocks_ref, panels_in, panels_ref, out_ref):
    rows = blocks_ref.shape[1]
    keep_panels((level - 1) * 2 * even_ref.shape[0], even_ref, odd_ref, panels_ref)
    for t in range(rows):
        row_sums(slots, level, blocks_ref.at[level - 1, t], panels_ref, out_ref, t)


def upper_solve(level, fwd_t_ref, diag_ref, parts):
    upper_t = fwd_t_ref[level]
    if parts:
        total = parts[0][...]
        for ref in parts[1:]:
            total = total + ref[...].astype(F32)
        upper_t = upper_t - total
    return dot(upper_t.astype(BF16), diag_ref[level, 0])


def backward_diag(level, count, *refs):
    parts, (fwd_t_ref, diag_ref), (out_ref, send_ref) = refs[:count], refs[count : count + 2], refs[-2:]
    out_t = upper_solve(level, fwd_t_ref, diag_ref, parts)
    rounded = out_t.astype(BF16)
    for i in range(send_ref.shape[0]):
        send_ref[i] = rounded
    out_ref[level, 0] = out_t.T


def last_diag_kernel(count, *refs):
    parts, (fwd_t_ref, diag_ref, out_in), (out_hbm, panel, sems) = refs[:count], refs[count:-3], refs[-3:]
    ready = out_in.shape[0] - 1
    early = pltpu.make_async_copy(out_in.at[pl.ds(1, ready)], out_hbm.at[pl.ds(1, ready)], sems.at[0])
    early.start()
    panel[0, 0] = upper_solve(0, fwd_t_ref, diag_ref, parts).T
    late = pltpu.make_async_copy(panel, out_hbm.at[pl.ds(0, 1)], sems.at[1])
    late.start()
    early.wait()
    late.wait()


def backward_sums_kernel(level, first, last, slots, panels_ref, blocks_ref, *refs):
    rows, per_row = blocks_ref.shape[1:3]
    width = blocks_ref.shape[4]
    if last:
        acc_in, even_ref, odd_ref, acc_ref = refs
        acc_ref[...] = acc_in[: acc_ref.shape[0]]
    else:
        acc_ref, even_ref, odd_ref = refs[-3:]
    if first:
        acc_ref[...] = jnp.zeros_like(acc_ref)
    for t in range(rows):
        right = jnp.concatenate([blocks_ref[level - 1, t, q] for q in range(per_row)], axis=1)
        terms = dot(panels_ref[t], right)
        for q in range(per_row):
            at = slots[level - 1, t * per_row + q]
            acc_ref[at] = acc_ref[at] + terms[:, q * width : (q + 1) * width]
    count = even_ref.shape[0]
    for i in range(count):
        at = (level - 1) * 2 * count + 2 * i
        even_ref[i] = acc_ref[at]
        odd_ref[i] = acc_ref[at + 1].astype(BF16)


def pair_kernel(even_ref, got_ref, own_ref, *send):
    own_ref[...] = even_ref[0] + got_ref[0].astype(F32)
    for i, ref in enumerate(send):
        ref[...] = (even_ref[i + 1] + got_ref[i + 1].astype(F32)).astype(BF16)


def swap(x, step):
    size = lax.axis_size("prow")
    return in_vmem(lax.ppermute(x, "prow", [(i, i ^ step) for i in range(size)]))


def per_device(right_side, blocks, pattern, diag_inverse):
    levels, panels_dev, order, width = right_side.shape
    rows, per_row = blocks.shape[1], blocks.shape[2]
    row_groups = lax.axis_size("prow")
    col_groups = lax.axis_size("pcol")
    level_rows = panels_dev * row_groups * col_groups
    within = pattern % level_rows
    home = (within // (level_rows // row_groups)) ^ lax.axis_index("prow")
    slots = (pattern // level_rows) * row_groups + home
    slots = in_vmem(slots.reshape(levels - 1, rows * per_row))
    full = pltpu.VMEM((levels, panels_dev, order, width), F32)
    fwd_t_shape = pltpu.VMEM((levels, width, order), F32)
    one = pltpu.VMEM((order, width), BF16)
    half = row_groups // 2
    far = half // 2
    backward_order = [far] + [i for i in reversed(range(1, half)) if i != far]
    forward_order = backward_order[::-1]
    evens_f = pltpu.VMEM((half, order, width), BF16)
    evens_b = pltpu.VMEM((half, width, order), F32)
    odds_b = pltpu.VMEM((half, width, order), BF16)
    send_xz = pltpu.VMEM((col_groups, width, order), BF16)
    sums_f = pltpu.VMEM((rows, order, width), BF16)
    panels_shape = pltpu.VMEM(((levels - 1) * row_groups, order, width), BF16)
    acc_shape = pltpu.VMEM(((levels - 1) * row_groups, width, order), F32)

    fwd, fwd_t, send = pl.pallas_call(
        first_diag_kernel,
        in_specs=[ANY, ANY],
        out_specs=[VM, VM, VM],
        out_shape=[full, fwd_t_shape, one],
        scratch_shapes=[
            pltpu.VMEM((order, width), F32),
            pltpu.VMEM((order, order), BF16),
            pltpu.SemaphoreType.DMA((2,)),
        ],
        compiler_params=params(8),
        name="first_diag",
    )(in_hbm(right_side), in_hbm(diag_inverse))
    blocks_hbm = in_hbm(blocks)
    blocks, right_side, diag_inverse = in_vmem(blocks), in_vmem(right_side), in_vmem(diag_inverse)
    panels = None
    for level in range(1, levels):
        last = level == levels - 1
        even = pl.pallas_call(
            functools.partial(pack_kernel, forward_order),
            in_specs=[VM] * half,
            out_specs=VM,
            out_shape=evens_f,
            compiler_params=params(2),
            name="pack",
        )(in_vmem(send), *[swap(send, 2 * i) for i in forward_order])
        odd = swap(even, 1)
        even = in_vmem(even)
        if level == 1:
            panels, parts = pl.pallas_call(
                first_sums_kernel,
                in_specs=[VM, VM, VM, ANY],
                out_specs=[VM, VM],
                out_shape=[panels_shape, sums_f],
                scratch_shapes=[
                    pltpu.VMEM((rows, per_row, order, order), BF16),
                    pltpu.SemaphoreType.DMA((4,)),
                ],
                compiler_params=params(8),
                name="first_sums",
            )(slots, even, odd, blocks_hbm)
        else:
            panels, parts = pl.pallas_call(
                functools.partial(forward_sums_kernel, level),
                in_specs=[VM, VM, VM, VM, VM],
                out_specs=[VM, VM],
                out_shape=[panels_shape, sums_f],
                input_output_aliases={4: 0},
                compiler_params=params(8),
                name="forward_sums",
            )(slots, even, odd, blocks, in_vmem(panels))
        parts = in_vmem(lax.all_to_all(parts, "pcol", 0, 0, tiled=True))
        made = pl.pallas_call(
            functools.partial(forward_diag_kernel, level),
            in_specs=[VM, VM, VM, VM, VM],
            out_specs=[VM, VM] if last else [VM, VM, VM],
            out_shape=[full, fwd_t_shape] + ([] if last else [one]),
            input_output_aliases={3: 0, 4: 1},
            compiler_params=params(8),
            name="forward_diag",
        )(parts, right_side, diag_inverse, in_vmem(fwd), in_vmem(fwd_t))
        fwd, fwd_t, send = made[0], made[1], made[-1]
    out = acc = parts = None
    for level in reversed(range(levels)):
        first = level == levels - 1
        if level == 0:
            out = pl.pallas_call(
                functools.partial(last_diag_kernel, half),
                in_specs=[VM] * (half + 3),
                out_specs=ANY,
                out_shape=pltpu.HBM(full.shape, F32),
                scratch_shapes=[
                    pltpu.VMEM((1,) + full.shape[1:], F32),
                    pltpu.SemaphoreType.DMA((2,)),
                ],
                compiler_params=params(8),
                name="last_diag",
            )(*parts, in_vmem(fwd_t), diag_inverse, in_vmem(out))
            break
        made = pl.pallas_call(
            functools.partial(backward_diag, level, 0 if first else half),
            in_specs=[VM, VM] if first else [VM] * (half + 3),
            out_specs=[VM, VM],
            out_shape=[full, send_xz],
            input_output_aliases={} if first else {half + 2: 0},
            compiler_params=params(8),
            name="backward_diag",
        )(*([] if first else parts), in_vmem(fwd_t), diag_inverse, *([] if first else [in_vmem(out)]))
        out = made[0]
        gathered = in_vmem(lax.all_to_all(made[1], "pcol", 0, 0, tiled=True))
        done = level == 1
        made = pl.pallas_call(
            functools.partial(backward_sums_kernel, level, first, done),
            in_specs=[VM, VM, VM] + ([] if first else [VM]),
            out_specs=[VM, VM] if done else [VM, VM, VM],
            out_shape=([] if done else [acc_shape]) + [evens_b, odds_b],
            scratch_shapes=[pltpu.VMEM((row_groups, width, order), F32)] if done else [],
            input_output_aliases={} if first or done else {3: 0},
            compiler_params=params(8),
            name="backward_sums",
        )(*([slots, gathered, blocks] + ([] if first else [in_vmem(acc)])))
        acc = made[0]
        made = pl.pallas_call(
            pair_kernel,
            in_specs=[VM, VM],
            out_specs=[VM] * half,
            out_shape=[pltpu.VMEM((width, order), F32)] + [pltpu.VMEM((width, order), BF16)] * (half - 1),
            compiler_params=params(2),
            name="pair",
        )(in_vmem(made[-2]), swap(made[-1], 1))
        parts = [in_vmem(made[0])] + [swap(made[i], 2 * i) for i in backward_order]
    return fwd, out


def solution(mesh):
    in_specs = (
        P(None, ("prow", "pcol"), None, None),
        P(None, "prow", "pcol", None, None),
        P(None, "prow", "pcol"),
        P(None, ("prow", "pcol"), None, None),
    )
    out_specs = (P(None, ("prow", "pcol"), None, None), P(None, ("prow", "pcol"), None, None))
    return jax.shard_map(
        per_device, mesh=mesh, in_specs=in_specs, out_specs=out_specs, check_vma=False
    )
```

```python
import functools

import jax
import jax.numpy as jnp
from jax import lax
from jax.experimental import pallas as pl
from jax.experimental.pallas import tpu as pltpu
from jax.sharding import PartitionSpec as P

F32 = jnp.float32
BF16 = jnp.bfloat16
VM = pl.BlockSpec(memory_space=pltpu.VMEM)
ANY = pl.BlockSpec(memory_space=pl.ANY)


def params(mib):
    return pltpu.CompilerParams(vmem_limit_bytes=mib * 1024 * 1024)


def in_vmem(x):
    return pltpu.with_memory_space_constraint(x, pltpu.VMEM)


def in_hbm(x):
    return pltpu.with_memory_space_constraint(x, pltpu.HBM)


def dot(a, b):
    return jnp.dot(a, b, preferred_element_type=F32)


def total_of(ref):
    total = ref[0].astype(F32)
    for i in range(1, ref.shape[0]):
        total = total + ref[i].astype(F32)
    return total


def finish_forward(level, lower_in, diag, fwd_ref, fwd_t_ref, *send):
    out = dot(diag, lower_in.astype(BF16))
    for send_ref in send:
        send_ref[...] = out.astype(BF16)
    fwd_ref[level, 0] = out
    fwd_t_ref[level] = out.T


def first_diag_kernel(right_hbm, diag_hbm, fwd_ref, fwd_t_ref, send_ref, right, diag, sems):
    copies = [
        pltpu.make_async_copy(right_hbm.at[0, 0], right, sems.at[0]),
        pltpu.make_async_copy(diag_hbm.at[0, 0], diag, sems.at[1]),
    ]
    for copy in copies:
        copy.start()
    for copy in copies:
        copy.wait()
    finish_forward(0, right[...], diag[...], fwd_ref, fwd_t_ref, send_ref)


def forward_diag_kernel(level, parts_ref, right_ref, diag_ref, fwd_in, fwd_t_in, fwd_ref, fwd_t_ref, *send):
    lower_in = right_ref[level, 0] - total_of(parts_ref)
    finish_forward(level, lower_in, diag_ref[level, 0], fwd_ref, fwd_t_ref, *send)


def row_sums(slots, level, blocks, panels_ref, out_ref, t):
    per_row = blocks.shape[0]
    left = jnp.concatenate([blocks[q] for q in range(per_row)], axis=1)
    at = [slots[level - 1, t * per_row + q] for q in range(per_row)]
    right = jnp.concatenate([panels_ref[i] for i in at], axis=0)
    out_ref[t] = dot(left, right).astype(BF16)


def pack_kernel(own_ref, other_ref, out_ref):
    out_ref[0] = own_ref[...]
    out_ref[1] = other_ref[...]


def keep_panels(at, order, pairs, panels_ref):
    for i, ref in zip([0] + order, pairs):
        panels_ref[at + 2 * i : at + 2 * i + 2] = ref[...]


def load_kernel(blocks_hbm, held, sem):
    copy = pltpu.make_async_copy(blocks_hbm.at[0], held, sem)
    copy.start()
    copy.wait()


def first_sums_kernel(order, slots, blocks_ref, *refs):
    pairs, (panels_ref, out_ref) = refs[:-2], refs[-2:]
    keep_panels(0, order, pairs, panels_ref)
    for t in range(blocks_ref.shape[0]):
        row_sums(slots, 1, blocks_ref.at[t], panels_ref, out_ref, t)


def forward_sums_kernel(level, order, slots, blocks_ref, panels_in, *refs):
    pairs, (panels_ref, out_ref) = refs[:-2], refs[-2:]
    rows = blocks_ref.shape[1]
    keep_panels((level - 1) * 2 * len(pairs), order, pairs, panels_ref)
    for t in range(rows):
        row_sums(slots, level, blocks_ref.at[level - 1, t], panels_ref, out_ref, t)


def upper_solve(level, fwd_t_ref, diag_ref, parts):
    upper_t = fwd_t_ref[level]
    if parts:
        total = parts[0][...]
        for ref in parts[1:]:
            total = total + ref[...].astype(F32)
        upper_t = upper_t - total
    return dot(upper_t.astype(BF16), diag_ref[level, 0])


def backward_diag(level, count, *refs):
    parts, (fwd_t_ref, diag_ref), (out_ref, send_ref) = refs[:count], refs[count : count + 2], refs[-2:]
    out_t = upper_solve(level, fwd_t_ref, diag_ref, parts)
    rounded = out_t.astype(BF16)
    for i in range(send_ref.shape[0]):
        send_ref[i] = rounded
    out_ref[level, 0] = out_t.T


def last_diag_kernel(count, *refs):
    parts, (fwd_t_ref, diag_ref, out_in), (out_hbm, panel, sems) = refs[:count], refs[count:-3], refs[-3:]
    ready = out_in.shape[0] - 1
    early = pltpu.make_async_copy(out_in.at[pl.ds(1, ready)], out_hbm.at[pl.ds(1, ready)], sems.at[0])
    early.start()
    panel[0, 0] = upper_solve(0, fwd_t_ref, diag_ref, parts).T
    late = pltpu.make_async_copy(panel, out_hbm.at[pl.ds(0, 1)], sems.at[1])
    late.start()
    early.wait()
    late.wait()


def backward_sums_kernel(level, first, last, slots, panels_ref, blocks_ref, *refs):
    rows, per_row = blocks_ref.shape[1:3]
    width = blocks_ref.shape[4]
    if last:
        acc_in, even_ref, odd_ref, acc_ref = refs
        acc_ref[...] = acc_in[: acc_ref.shape[0]]
    else:
        acc_ref, even_ref, odd_ref = refs[-3:]
    if first:
        acc_ref[...] = jnp.zeros_like(acc_ref)
    for t in range(rows):
        right = jnp.concatenate([blocks_ref[level - 1, t, q] for q in range(per_row)], axis=1)
        terms = dot(panels_ref[t], right)
        for q in range(per_row):
            at = slots[level - 1, t * per_row + q]
            acc_ref[at] = acc_ref[at] + terms[:, q * width : (q + 1) * width]
    count = even_ref.shape[0]
    for i in range(count):
        at = (level - 1) * 2 * count + 2 * i
        even_ref[i] = acc_ref[at]
        odd_ref[i] = acc_ref[at + 1].astype(BF16)


def pair_kernel(even_ref, got_ref, own_ref, *send):
    own_ref[...] = even_ref[0] + got_ref[0].astype(F32)
    for i, ref in enumerate(send):
        ref[...] = (even_ref[i + 1] + got_ref[i + 1].astype(F32)).astype(BF16)


def swap(x, step):
    size = lax.axis_size("prow")
    return in_vmem(lax.ppermute(x, "prow", [(i, i ^ step) for i in range(size)]))


def per_device(right_side, blocks, pattern, diag_inverse):
    levels, panels_dev, order, width = right_side.shape
    rows, per_row = blocks.shape[1], blocks.shape[2]
    row_groups = lax.axis_size("prow")
    col_groups = lax.axis_size("pcol")
    level_rows = panels_dev * row_groups * col_groups
    within = pattern % level_rows
    home = (within // (level_rows // row_groups)) ^ lax.axis_index("prow")
    slots = (pattern // level_rows) * row_groups + home
    slots = in_vmem(slots.reshape(levels - 1, rows * per_row))
    full = pltpu.VMEM((levels, panels_dev, order, width), F32)
    fwd_t_shape = pltpu.VMEM((levels, width, order), F32)
    one = pltpu.VMEM((order, width), BF16)
    half = row_groups // 2
    far = half // 2
    backward_order = [far] + [i for i in reversed(range(1, half)) if i != far]
    forward_order = backward_order[::-1]
    evens_b = pltpu.VMEM((half, width, order), F32)
    odds_b = pltpu.VMEM((half, width, order), BF16)
    send_xz = pltpu.VMEM((col_groups, width, order), BF16)
    sums_f = pltpu.VMEM((rows, order, width), BF16)
    panels_shape = pltpu.VMEM(((levels - 1) * row_groups, order, width), BF16)
    acc_shape = pltpu.VMEM(((levels - 1) * row_groups, width, order), F32)

    fwd, fwd_t, send = pl.pallas_call(
        first_diag_kernel,
        in_specs=[ANY, ANY],
        out_specs=[VM, VM, VM],
        out_shape=[full, fwd_t_shape, one],
        scratch_shapes=[
            pltpu.VMEM((order, width), F32),
            pltpu.VMEM((order, order), BF16),
            pltpu.SemaphoreType.DMA((2,)),
        ],
        compiler_params=params(8),
        name="first_diag",
    )(in_hbm(right_side), in_hbm(diag_inverse))
    first_blocks = in_vmem(
        pl.pallas_call(
            load_kernel,
            in_specs=[ANY],
            out_specs=ANY,
            out_shape=pltpu.VMEM(blocks.shape[1:], BF16),
            scratch_shapes=[pltpu.SemaphoreType.DMA(())],
            compiler_params=params(2),
            cost_estimate=pl.CostEstimate(
                flops=0, bytes_accessed=2 * blocks[0].size, transcendentals=0
            ),
            name="load",
        )(in_hbm(blocks))
    )
    blocks, right_side, diag_inverse = in_vmem(blocks), in_vmem(right_side), in_vmem(diag_inverse)
    panels = None
    for level in range(1, levels):
        last = level == levels - 1
        pair = pl.pallas_call(
            pack_kernel,
            in_specs=[VM, VM],
            out_specs=VM,
            out_shape=pltpu.VMEM((2, order, width), BF16),
            compiler_params=params(2),
            name="pack",
        )(in_vmem(send), swap(send, 1))
        pairs = [in_vmem(pair)] + [swap(pair, 2 * i) for i in forward_order]
        if level == 1:
            panels, parts = pl.pallas_call(
                functools.partial(first_sums_kernel, forward_order),
                in_specs=[VM, VM] + [VM] * half,
                out_specs=[VM, VM],
                out_shape=[panels_shape, sums_f],
                compiler_params=params(8),
                name="first_sums",
            )(slots, first_blocks, *pairs)
        else:
            panels, parts = pl.pallas_call(
                functools.partial(forward_sums_kernel, level, forward_order),
                in_specs=[VM] * (half + 3),
                out_specs=[VM, VM],
                out_shape=[panels_shape, sums_f],
                input_output_aliases={2: 0},
                compiler_params=params(8),
                name="forward_sums",
            )(slots, blocks, in_vmem(panels), *pairs)
        parts = in_vmem(lax.all_to_all(parts, "pcol", 0, 0, tiled=True))
        made = pl.pallas_call(
            functools.partial(forward_diag_kernel, level),
            in_specs=[VM, VM, VM, VM, VM],
            out_specs=[VM, VM] if last else [VM, VM, VM],
            out_shape=[full, fwd_t_shape] + ([] if last else [one]),
            input_output_aliases={3: 0, 4: 1},
            compiler_params=params(8),
            name="forward_diag",
        )(parts, right_side, diag_inverse, in_vmem(fwd), in_vmem(fwd_t))
        fwd, fwd_t, send = made[0], made[1], made[-1]
    out = acc = parts = None
    for level in reversed(range(levels)):
        first = level == levels - 1
        if level == 0:
            out = pl.pallas_call(
                functools.partial(last_diag_kernel, half),
                in_specs=[VM] * (half + 3),
                out_specs=ANY,
                out_shape=pltpu.HBM(full.shape, F32),
                scratch_shapes=[
                    pltpu.VMEM((1,) + full.shape[1:], F32),
                    pltpu.SemaphoreType.DMA((2,)),
                ],
                compiler_params=params(8),
                name="last_diag",
            )(*parts, in_vmem(fwd_t), diag_inverse, in_vmem(out))
            break
        made = pl.pallas_call(
            functools.partial(backward_diag, level, 0 if first else half),
            in_specs=[VM, VM] if first else [VM] * (half + 3),
            out_specs=[VM, VM],
            out_shape=[full, send_xz],
            input_output_aliases={} if first else {half + 2: 0},
            compiler_params=params(8),
            name="backward_diag",
        )(*([] if first else parts), in_vmem(fwd_t), diag_inverse, *([] if first else [in_vmem(out)]))
        out = made[0]
        gathered = in_vmem(lax.all_to_all(made[1], "pcol", 0, 0, tiled=True))
        done = level == 1
        made = pl.pallas_call(
            functools.partial(backward_sums_kernel, level, first, done),
            in_specs=[VM, VM, VM] + ([] if first else [VM]),
            out_specs=[VM, VM] if done else [VM, VM, VM],
            out_shape=([] if done else [acc_shape]) + [evens_b, odds_b],
            scratch_shapes=[pltpu.VMEM((row_groups, width, order), F32)] if done else [],
            input_output_aliases={} if first or done else {3: 0},
            compiler_params=params(8),
            name="backward_sums",
        )(*([slots, gathered, blocks] + ([] if first else [in_vmem(acc)])))
        acc = made[0]
        made = pl.pallas_call(
            pair_kernel,
            in_specs=[VM, VM],
            out_specs=[VM] * half,
            out_shape=[pltpu.VMEM((width, order), F32)] + [pltpu.VMEM((width, order), BF16)] * (half - 1),
            compiler_params=params(2),
            name="pair",
        )(in_vmem(made[-2]), swap(made[-1], 1))
        parts = [in_vmem(made[0])] + [swap(made[i], 2 * i) for i in backward_order]
    return fwd, out


def solution(mesh):
    in_specs = (
        P(None, ("prow", "pcol"), None, None),
        P(None, "prow", "pcol", None, None),
        P(None, "prow", "pcol"),
        P(None, ("prow", "pcol"), None, None),
    )
    out_specs = (P(None, ("prow", "pcol"), None, None), P(None, ("prow", "pcol"), None, None))
    return jax.shard_map(
        per_device, mesh=mesh, in_specs=in_specs, out_specs=out_specs, check_vma=False
    )
```

```python
import functools

import jax
import jax.numpy as jnp
from jax import lax
from jax.experimental import pallas as pl
from jax.experimental.pallas import tpu as pltpu
from jax.sharding import PartitionSpec as P

F32 = jnp.float32
BF16 = jnp.bfloat16
VM = pl.BlockSpec(memory_space=pltpu.VMEM)
ANY = pl.BlockSpec(memory_space=pl.ANY)


def params(mib):
    return pltpu.CompilerParams(vmem_limit_bytes=mib * 1024 * 1024)


def in_vmem(x):
    return pltpu.with_memory_space_constraint(x, pltpu.VMEM)


def in_hbm(x):
    return pltpu.with_memory_space_constraint(x, pltpu.HBM)


def dot(a, b):
    return jnp.dot(a, b, preferred_element_type=F32)


def total_of(ref):
    total = ref[0].astype(F32)
    for i in range(1, ref.shape[0]):
        total = total + ref[i].astype(F32)
    return total


def finish_forward(level, lower_in, diag, fwd_ref, fwd_t_ref, *send):
    out = dot(diag, lower_in.astype(BF16))
    for send_ref in send:
        send_ref[...] = out.astype(BF16)
    fwd_ref[level, 0] = out
    fwd_t_ref[level] = out.T


def first_diag_kernel(right_hbm, diag_hbm, fwd_ref, fwd_t_ref, send_ref, right, diag, sems):
    copies = [
        pltpu.make_async_copy(right_hbm.at[0, 0], right, sems.at[0]),
        pltpu.make_async_copy(diag_hbm.at[0, 0], diag, sems.at[1]),
    ]
    for copy in copies:
        copy.start()
    for copy in copies:
        copy.wait()
    finish_forward(0, right[...], diag[...], fwd_ref, fwd_t_ref, send_ref)


def forward_diag_kernel(level, parts_ref, right_ref, diag_ref, fwd_in, fwd_t_in, fwd_ref, fwd_t_ref, *send):
    lower_in = right_ref[level, 0] - total_of(parts_ref)
    finish_forward(level, lower_in, diag_ref[level, 0], fwd_ref, fwd_t_ref, *send)


def row_sums(slots, level, blocks, panels_ref, out_ref, t):
    per_row = blocks.shape[0]
    left = jnp.concatenate([blocks[q] for q in range(per_row)], axis=1)
    at = [slots[level - 1, t * per_row + q] for q in range(per_row)]
    right = jnp.concatenate([panels_ref[i] for i in at], axis=0)
    out_ref[t] = dot(left, right).astype(BF16)


def pack_kernel(own_ref, other_ref, out_ref):
    out_ref[0] = own_ref[...]
    out_ref[1] = other_ref[...]


def keep_panels(at, order, pairs, panels_ref):
    for i, ref in zip([0] + order, pairs):
        panels_ref[at + 2 * i : at + 2 * i + 2] = ref[...]


def load_kernel(blocks_hbm, held, sem):
    copy = pltpu.make_async_copy(blocks_hbm.at[0], held, sem)
    copy.start()
    copy.wait()


def first_sums_kernel(order, slots, blocks_ref, *refs):
    pairs, (panels_ref, out_ref) = refs[:-2], refs[-2:]
    keep_panels(0, order, pairs, panels_ref)
    for t in range(blocks_ref.shape[0]):
        row_sums(slots, 1, blocks_ref.at[t], panels_ref, out_ref, t)


def forward_sums_kernel(level, order, slots, blocks_ref, panels_in, *refs):
    pairs, (panels_ref, out_ref) = refs[:-2], refs[-2:]
    rows = blocks_ref.shape[1]
    keep_panels((level - 1) * 2 * len(pairs), order, pairs, panels_ref)
    for t in range(rows):
        row_sums(slots, level, blocks_ref.at[level - 1, t], panels_ref, out_ref, t)


def upper_solve(level, fwd_t_ref, diag_ref, parts):
    upper_t = fwd_t_ref[level]
    if parts:
        total = parts[0][...]
        for ref in parts[1:]:
            total = total + ref[...].astype(F32)
        upper_t = upper_t - total
    return dot(upper_t.astype(BF16), diag_ref[level, 0])


def backward_diag(level, count, *refs):
    parts, (fwd_t_ref, diag_ref), (out_ref, send_ref) = refs[:count], refs[count : count + 2], refs[-2:]
    out_t = upper_solve(level, fwd_t_ref, diag_ref, parts)
    rounded = out_t.astype(BF16)
    for i in range(send_ref.shape[0]):
        send_ref[i] = rounded
    out_ref[level, 0] = out_t.T


def last_diag_kernel(count, *refs):
    parts, (fwd_t_ref, diag_ref, out_in), (out_hbm, panel, sems) = refs[:count], refs[count:-3], refs[-3:]
    ready = out_in.shape[0] - 1
    early = pltpu.make_async_copy(out_in.at[pl.ds(1, ready)], out_hbm.at[pl.ds(1, ready)], sems.at[0])
    early.start()
    panel[0, 0] = upper_solve(0, fwd_t_ref, diag_ref, parts).T
    late = pltpu.make_async_copy(panel, out_hbm.at[pl.ds(0, 1)], sems.at[1])
    late.start()
    early.wait()
    late.wait()


def backward_sums_kernel(level, first, last, slots, panels_ref, blocks_ref, *refs):
    rows, per_row = blocks_ref.shape[1:3]
    width = blocks_ref.shape[4]
    if last:
        acc_in, even_ref, odd_ref, acc_ref = refs
        acc_ref[...] = acc_in[: acc_ref.shape[0]]
    else:
        acc_ref, even_ref, odd_ref = refs[-3:]
    if first:
        acc_ref[...] = jnp.zeros_like(acc_ref)
    for t in range(rows):
        right = jnp.concatenate([blocks_ref[level - 1, t, q] for q in range(per_row)], axis=1)
        terms = dot(panels_ref[t], right)
        for q in range(per_row):
            at = slots[level - 1, t * per_row + q]
            acc_ref[at] = acc_ref[at] + terms[:, q * width : (q + 1) * width]
    count = even_ref.shape[0]
    for i in range(count):
        at = (level - 1) * 2 * count + 2 * i
        even_ref[i] = acc_ref[at]
        odd_ref[i] = acc_ref[at + 1].astype(BF16)


def pair_kernel(even_ref, got_ref, own_ref, *send):
    own_ref[...] = even_ref[0] + got_ref[0].astype(F32)
    for i, ref in enumerate(send):
        ref[...] = (even_ref[i + 1] + got_ref[i + 1].astype(F32)).astype(BF16)


def swap(x, step):
    size = lax.axis_size("prow")
    return in_vmem(lax.ppermute(x, "prow", [(i, i ^ step) for i in range(size)]))


def per_device(right_side, blocks, pattern, diag_inverse):
    levels, panels_dev, order, width = right_side.shape
    rows, per_row = blocks.shape[1], blocks.shape[2]
    row_groups = lax.axis_size("prow")
    col_groups = lax.axis_size("pcol")
    level_rows = panels_dev * row_groups * col_groups
    within = pattern % level_rows
    home = (within // (level_rows // row_groups)) ^ lax.axis_index("prow")
    slots = (pattern // level_rows) * row_groups + home
    slots = in_vmem(slots.reshape(levels - 1, rows * per_row))
    full = pltpu.VMEM((levels, panels_dev, order, width), F32)
    fwd_t_shape = pltpu.VMEM((levels, width, order), F32)
    one = pltpu.VMEM((order, width), BF16)
    half = row_groups // 2
    far = half // 2
    backward_order = [far] + [i for i in reversed(range(1, half)) if i != far]
    forward_order = list(range(1, half))
    evens_b = pltpu.VMEM((half, width, order), F32)
    odds_b = pltpu.VMEM((half, width, order), BF16)
    send_xz = pltpu.VMEM((col_groups, width, order), BF16)
    sums_f = pltpu.VMEM((rows, order, width), BF16)
    panels_shape = pltpu.VMEM(((levels - 1) * row_groups, order, width), BF16)
    acc_shape = pltpu.VMEM(((levels - 1) * row_groups, width, order), F32)

    fwd, fwd_t, send = pl.pallas_call(
        first_diag_kernel,
        in_specs=[ANY, ANY],
        out_specs=[VM, VM, VM],
        out_shape=[full, fwd_t_shape, one],
        scratch_shapes=[
            pltpu.VMEM((order, width), F32),
            pltpu.VMEM((order, order), BF16),
            pltpu.SemaphoreType.DMA((2,)),
        ],
        compiler_params=params(8),
        name="first_diag",
    )(in_hbm(right_side), in_hbm(diag_inverse))
    first_blocks = in_vmem(
        pl.pallas_call(
            load_kernel,
            in_specs=[ANY],
            out_specs=ANY,
            out_shape=pltpu.VMEM(blocks.shape[1:], BF16),
            scratch_shapes=[pltpu.SemaphoreType.DMA(())],
            compiler_params=params(2),
            cost_estimate=pl.CostEstimate(
                flops=0, bytes_accessed=2 * blocks[0].size, transcendentals=0
            ),
            name="load",
        )(in_hbm(blocks))
    )
    blocks, right_side, diag_inverse = in_vmem(blocks), in_vmem(right_side), in_vmem(diag_inverse)
    panels = None
    for level in range(1, levels):
        last = level == levels - 1
        pair = pl.pallas_call(
            pack_kernel,
            in_specs=[VM, VM],
            out_specs=VM,
            out_shape=pltpu.VMEM((2, order, width), BF16),
            compiler_params=params(2),
            name="pack",
        )(in_vmem(send), swap(send, 1))
        pairs = [in_vmem(pair)] + [swap(pair, 2 * i) for i in forward_order]
        if level == 1:
            panels, parts = pl.pallas_call(
                functools.partial(first_sums_kernel, forward_order),
                in_specs=[VM, VM] + [VM] * half,
                out_specs=[VM, VM],
                out_shape=[panels_shape, sums_f],
                compiler_params=params(8),
                name="first_sums",
            )(slots, first_blocks, *pairs)
        else:
            panels, parts = pl.pallas_call(
                functools.partial(forward_sums_kernel, level, forward_order),
                in_specs=[VM] * (half + 3),
                out_specs=[VM, VM],
                out_shape=[panels_shape, sums_f],
                input_output_aliases={2: 0},
                compiler_params=params(8),
                name="forward_sums",
            )(slots, blocks, in_vmem(panels), *pairs)
        parts = in_vmem(lax.all_to_all(parts, "pcol", 0, 0, tiled=True))
        made = pl.pallas_call(
            functools.partial(forward_diag_kernel, level),
            in_specs=[VM, VM, VM, VM, VM],
            out_specs=[VM, VM] if last else [VM, VM, VM],
            out_shape=[full, fwd_t_shape] + ([] if last else [one]),
            input_output_aliases={3: 0, 4: 1},
            compiler_params=params(8),
            name="forward_diag",
        )(parts, right_side, diag_inverse, in_vmem(fwd), in_vmem(fwd_t))
        fwd, fwd_t, send = made[0], made[1], made[-1]
    out = acc = parts = None
    for level in reversed(range(levels)):
        first = level == levels - 1
        if level == 0:
            out = pl.pallas_call(
                functools.partial(last_diag_kernel, half),
                in_specs=[VM] * (half + 3),
                out_specs=ANY,
                out_shape=pltpu.HBM(full.shape, F32),
                scratch_shapes=[
                    pltpu.VMEM((1,) + full.shape[1:], F32),
                    pltpu.SemaphoreType.DMA((2,)),
                ],
                compiler_params=params(8),
                name="last_diag",
            )(*parts, in_vmem(fwd_t), diag_inverse, in_vmem(out))
            break
        made = pl.pallas_call(
            functools.partial(backward_diag, level, 0 if first else half),
            in_specs=[VM, VM] if first else [VM] * (half + 3),
            out_specs=[VM, VM],
            out_shape=[full, send_xz],
            input_output_aliases={} if first else {half + 2: 0},
            compiler_params=params(8),
            name="backward_diag",
        )(*([] if first else parts), in_vmem(fwd_t), diag_inverse, *([] if first else [in_vmem(out)]))
        out = made[0]
        gathered = in_vmem(lax.all_to_all(made[1], "pcol", 0, 0, tiled=True))
        done = level == 1
        made = pl.pallas_call(
            functools.partial(backward_sums_kernel, level, first, done),
            in_specs=[VM, VM, VM] + ([] if first else [VM]),
            out_specs=[VM, VM] if done else [VM, VM, VM],
            out_shape=([] if done else [acc_shape]) + [evens_b, odds_b],
            scratch_shapes=[pltpu.VMEM((row_groups, width, order), F32)] if done else [],
            input_output_aliases={} if first or done else {3: 0},
            compiler_params=params(8),
            name="backward_sums",
        )(*([slots, gathered, blocks] + ([] if first else [in_vmem(acc)])))
        acc = made[0]
        made = pl.pallas_call(
            pair_kernel,
            in_specs=[VM, VM],
            out_specs=[VM] * half,
            out_shape=[pltpu.VMEM((width, order), F32)] + [pltpu.VMEM((width, order), BF16)] * (half - 1),
            compiler_params=params(2),
            name="pair",
        )(in_vmem(made[-2]), swap(made[-1], 1))
        parts = [in_vmem(made[0])] + [swap(made[i], 2 * i) for i in backward_order]
    return fwd, out


def solution(mesh):
    in_specs = (
        P(None, ("prow", "pcol"), None, None),
        P(None, "prow", "pcol", None, None),
        P(None, "prow", "pcol"),
        P(None, ("prow", "pcol"), None, None),
    )
    out_specs = (P(None, ("prow", "pcol"), None, None), P(None, ("prow", "pcol"), None, None))
    return jax.shard_map(
        per_device, mesh=mesh, in_specs=in_specs, out_specs=out_specs, check_vma=False
    )
```

```python
import functools

import jax
import jax.numpy as jnp
from jax import lax
from jax.experimental import pallas as pl
from jax.experimental.pallas import tpu as pltpu
from jax.sharding import PartitionSpec as P

F32 = jnp.float32
BF16 = jnp.bfloat16
VM = pl.BlockSpec(memory_space=pltpu.VMEM)
ANY = pl.BlockSpec(memory_space=pl.ANY)


def params(mib):
    return pltpu.CompilerParams(vmem_limit_bytes=mib * 1024 * 1024)


def in_vmem(x):
    return pltpu.with_memory_space_constraint(x, pltpu.VMEM)


def in_hbm(x):
    return pltpu.with_memory_space_constraint(x, pltpu.HBM)


def dot(a, b):
    return jnp.dot(a, b, preferred_element_type=F32)


def total_of(ref):
    total = ref[0].astype(F32)
    for i in range(1, ref.shape[0]):
        total = total + ref[i].astype(F32)
    return total


def finish_forward(level, lower_in, diag, fwd_ref, fwd_t_ref, *send):
    out = dot(diag, lower_in.astype(BF16))
    for send_ref in send:
        send_ref[...] = out.astype(BF16)
    fwd_ref[level, 0] = out
    fwd_t_ref[level] = out.T


def first_diag_kernel(right_hbm, diag_hbm, fwd_ref, fwd_t_ref, send_ref, right, diag, sems):
    copies = [
        pltpu.make_async_copy(right_hbm.at[0, 0], right, sems.at[0]),
        pltpu.make_async_copy(diag_hbm.at[0, 0], diag, sems.at[1]),
    ]
    for copy in copies:
        copy.start()
    for copy in copies:
        copy.wait()
    finish_forward(0, right[...], diag[...], fwd_ref, fwd_t_ref, send_ref)


def forward_diag_kernel(level, parts_ref, right_ref, diag_ref, fwd_in, fwd_t_in, fwd_ref, fwd_t_ref, *send):
    lower_in = right_ref[level, 0] - total_of(parts_ref)
    finish_forward(level, lower_in, diag_ref[level, 0], fwd_ref, fwd_t_ref, *send)


def row_sums(slots, level, blocks, panels_ref, out_ref, t):
    per_row = blocks.shape[0]
    left = jnp.concatenate([blocks[q] for q in range(per_row)], axis=1)
    at = [slots[level - 1, t * per_row + q] for q in range(per_row)]
    right = jnp.concatenate([panels_ref[i] for i in at], axis=0)
    out_ref[t] = dot(left, right).astype(BF16)


def pack_kernel(own_ref, other_ref, out_ref):
    out_ref[0] = own_ref[...]
    out_ref[1] = other_ref[...]


def keep_panels(at, order, pairs, panels_ref):
    for i, ref in zip([0] + order, pairs):
        panels_ref[at + 2 * i : at + 2 * i + 2] = ref[...]


def load_kernel(blocks_hbm, held, sem):
    copy = pltpu.make_async_copy(blocks_hbm.at[0], held, sem)
    copy.start()
    copy.wait()


def first_sums_kernel(order, slots, blocks_ref, *refs):
    pairs, (panels_ref, out_ref) = refs[:-2], refs[-2:]
    keep_panels(0, order, pairs, panels_ref)
    for t in range(blocks_ref.shape[0]):
        row_sums(slots, 1, blocks_ref.at[t], panels_ref, out_ref, t)


def forward_sums_kernel(level, order, slots, blocks_ref, panels_in, *refs):
    pairs, (panels_ref, out_ref) = refs[:-2], refs[-2:]
    rows = blocks_ref.shape[1]
    keep_panels((level - 1) * 2 * len(pairs), order, pairs, panels_ref)
    for t in range(rows):
        row_sums(slots, level, blocks_ref.at[level - 1, t], panels_ref, out_ref, t)


def upper_solve(level, fwd_t_ref, diag_ref, parts):
    upper_t = fwd_t_ref[level]
    if parts:
        total = parts[0][...]
        for ref in parts[1:]:
            total = total + ref[...].astype(F32)
        upper_t = upper_t - total
    return dot(upper_t.astype(BF16), diag_ref[level, 0])


def backward_diag(level, count, *refs):
    parts, (fwd_t_ref, diag_ref), (out_ref, send_ref) = refs[:count], refs[count : count + 2], refs[-2:]
    out_t = upper_solve(level, fwd_t_ref, diag_ref, parts)
    rounded = out_t.astype(BF16)
    for i in range(send_ref.shape[0]):
        send_ref[i] = rounded
    out_ref[level, 0] = out_t.T


def last_diag_kernel(count, *refs):
    parts, (fwd_t_ref, diag_ref, out_in), (out_hbm, panel, sems) = refs[:count], refs[count:-3], refs[-3:]
    ready = out_in.shape[0] - 1
    early = pltpu.make_async_copy(out_in.at[pl.ds(1, ready)], out_hbm.at[pl.ds(1, ready)], sems.at[0])
    early.start()
    panel[0, 0] = upper_solve(0, fwd_t_ref, diag_ref, parts).T
    late = pltpu.make_async_copy(panel, out_hbm.at[pl.ds(0, 1)], sems.at[1])
    late.start()
    early.wait()
    late.wait()


def backward_sums_kernel(level, first, last, slots, panels_ref, blocks_ref, *refs):
    rows, per_row = blocks_ref.shape[1:3]
    width = blocks_ref.shape[4]
    if last:
        acc_in, even_ref, odd_ref, acc_ref = refs
        acc_ref[...] = acc_in[: acc_ref.shape[0]]
    else:
        acc_ref, even_ref, odd_ref = refs[-3:]
    if first:
        acc_ref[...] = jnp.zeros_like(acc_ref)
    for t in range(rows):
        right = jnp.concatenate([blocks_ref[level - 1, t, q] for q in range(per_row)], axis=1)
        terms = dot(panels_ref[t], right)
        for q in range(per_row):
            at = slots[level - 1, t * per_row + q]
            acc_ref[at] = acc_ref[at] + terms[:, q * width : (q + 1) * width]
    count = even_ref.shape[0]
    for i in range(count):
        at = (level - 1) * 2 * count + 2 * i
        even_ref[i] = acc_ref[at]
        odd_ref[i] = acc_ref[at + 1].astype(BF16)


def pair_kernel(even_ref, got_ref, own_ref, *send):
    own_ref[...] = even_ref[0] + got_ref[0].astype(F32)
    for i, ref in enumerate(send):
        ref[...] = (even_ref[i + 1] + got_ref[i + 1].astype(F32)).astype(BF16)


def swap(x, step):
    size = lax.axis_size("prow")
    return in_vmem(lax.ppermute(x, "prow", [(i, i ^ step) for i in range(size)]))


def per_device(right_side, blocks, pattern, diag_inverse):
    levels, panels_dev, order, width = right_side.shape
    rows, per_row = blocks.shape[1], blocks.shape[2]
    row_groups = lax.axis_size("prow")
    col_groups = lax.axis_size("pcol")
    level_rows = panels_dev * row_groups * col_groups
    within = pattern % level_rows
    home = (within // (level_rows // row_groups)) ^ lax.axis_index("prow")
    slots = (pattern // level_rows) * row_groups + home
    slots = in_vmem(slots.reshape(levels - 1, rows * per_row))
    full = pltpu.VMEM((levels, panels_dev, order, width), F32)
    fwd_t_shape = pltpu.VMEM((levels, width, order), F32)
    one = pltpu.VMEM((order, width), BF16)
    half = row_groups // 2
    backward_order = list(reversed(range(1, half)))
    forward_order = list(range(1, half))
    evens_b = pltpu.VMEM((half, width, order), F32)
    odds_b = pltpu.VMEM((half, width, order), BF16)
    send_xz = pltpu.VMEM((col_groups, width, order), BF16)
    sums_f = pltpu.VMEM((rows, order, width), BF16)
    panels_shape = pltpu.VMEM(((levels - 1) * row_groups, order, width), BF16)
    acc_shape = pltpu.VMEM(((levels - 1) * row_groups, width, order), F32)

    fwd, fwd_t, send = pl.pallas_call(
        first_diag_kernel,
        in_specs=[ANY, ANY],
        out_specs=[VM, VM, VM],
        out_shape=[full, fwd_t_shape, one],
        scratch_shapes=[
            pltpu.VMEM((order, width), F32),
            pltpu.VMEM((order, order), BF16),
            pltpu.SemaphoreType.DMA((2,)),
        ],
        compiler_params=params(8),
        name="first_diag",
    )(in_hbm(right_side), in_hbm(diag_inverse))
    first_blocks = in_vmem(
        pl.pallas_call(
            load_kernel,
            in_specs=[ANY],
            out_specs=ANY,
            out_shape=pltpu.VMEM(blocks.shape[1:], BF16),
            scratch_shapes=[pltpu.SemaphoreType.DMA(())],
            compiler_params=params(2),
            cost_estimate=pl.CostEstimate(
                flops=0, bytes_accessed=2 * blocks[0].size, transcendentals=0
            ),
            name="load",
        )(in_hbm(blocks))
    )
    blocks, right_side, diag_inverse = in_vmem(blocks), in_vmem(right_side), in_vmem(diag_inverse)
    panels = None
    for level in range(1, levels):
        last = level == levels - 1
        pair = pl.pallas_call(
            pack_kernel,
            in_specs=[VM, VM],
            out_specs=VM,
            out_shape=pltpu.VMEM((2, order, width), BF16),
            compiler_params=params(2),
            name="pack",
        )(in_vmem(send), swap(send, 1))
        pairs = [in_vmem(pair)] + [swap(pair, 2 * i) for i in forward_order]
        if level == 1:
            panels, parts = pl.pallas_call(
                functools.partial(first_sums_kernel, forward_order),
                in_specs=[VM, VM] + [VM] * half,
                out_specs=[VM, VM],
                out_shape=[panels_shape, sums_f],
                compiler_params=params(8),
                name="first_sums",
            )(slots, first_blocks, *pairs)
        else:
            panels, parts = pl.pallas_call(
                functools.partial(forward_sums_kernel, level, forward_order),
                in_specs=[VM] * (half + 3),
                out_specs=[VM, VM],
                out_shape=[panels_shape, sums_f],
                input_output_aliases={2: 0},
                compiler_params=params(8),
                name="forward_sums",
            )(slots, blocks, in_vmem(panels), *pairs)
        parts = in_vmem(lax.all_to_all(parts, "pcol", 0, 0, tiled=True))
        made = pl.pallas_call(
            functools.partial(forward_diag_kernel, level),
            in_specs=[VM, VM, VM, VM, VM],
            out_specs=[VM, VM] if last else [VM, VM, VM],
            out_shape=[full, fwd_t_shape] + ([] if last else [one]),
            input_output_aliases={3: 0, 4: 1},
            compiler_params=params(8),
            name="forward_diag",
        )(parts, right_side, diag_inverse, in_vmem(fwd), in_vmem(fwd_t))
        fwd, fwd_t, send = made[0], made[1], made[-1]
    out = acc = parts = None
    for level in reversed(range(levels)):
        first = level == levels - 1
        if level == 0:
            out = pl.pallas_call(
                functools.partial(last_diag_kernel, half),
                in_specs=[VM] * (half + 3),
                out_specs=ANY,
                out_shape=pltpu.HBM(full.shape, F32),
                scratch_shapes=[
                    pltpu.VMEM((1,) + full.shape[1:], F32),
                    pltpu.SemaphoreType.DMA((2,)),
                ],
                compiler_params=params(8),
                name="last_diag",
            )(*parts, in_vmem(fwd_t), diag_inverse, in_vmem(out))
            break
        made = pl.pallas_call(
            functools.partial(backward_diag, level, 0 if first else half),
            in_specs=[VM, VM] if first else [VM] * (half + 3),
            out_specs=[VM, VM],
            out_shape=[full, send_xz],
            input_output_aliases={} if first else {half + 2: 0},
            compiler_params=params(8),
            name="backward_diag",
        )(*([] if first else parts), in_vmem(fwd_t), diag_inverse, *([] if first else [in_vmem(out)]))
        out = made[0]
        gathered = in_vmem(lax.all_to_all(made[1], "pcol", 0, 0, tiled=True))
        done = level == 1
        made = pl.pallas_call(
            functools.partial(backward_sums_kernel, level, first, done),
            in_specs=[VM, VM, VM] + ([] if first else [VM]),
            out_specs=[VM, VM] if done else [VM, VM, VM],
            out_shape=([] if done else [acc_shape]) + [evens_b, odds_b],
            scratch_shapes=[pltpu.VMEM((row_groups, width, order), F32)] if done else [],
            input_output_aliases={} if first or done else {3: 0},
            compiler_params=params(8),
            name="backward_sums",
        )(*([slots, gathered, blocks] + ([] if first else [in_vmem(acc)])))
        acc = made[0]
        made = pl.pallas_call(
            pair_kernel,
            in_specs=[VM, VM],
            out_specs=[VM] * half,
            out_shape=[pltpu.VMEM((width, order), F32)] + [pltpu.VMEM((width, order), BF16)] * (half - 1),
            compiler_params=params(2),
            name="pair",
        )(in_vmem(made[-2]), swap(made[-1], 1))
        parts = [in_vmem(made[0])] + [swap(made[i], 2 * i) for i in backward_order]
    return fwd, out


def solution(mesh):
    in_specs = (
        P(None, ("prow", "pcol"), None, None),
        P(None, "prow", "pcol", None, None),
        P(None, "prow", "pcol"),
        P(None, ("prow", "pcol"), None, None),
    )
    out_specs = (P(None, ("prow", "pcol"), None, None), P(None, ("prow", "pcol"), None, None))
    return jax.shard_map(
        per_device, mesh=mesh, in_specs=in_specs, out_specs=out_specs, check_vma=False
    )
```
